32 devices in a mesh: group: 2 (over y), tile: 4 (over z), tm: 2 (over x), pol: 2 (over core).
Axes of the slice: x: 2, y: 2, z: 4, core: 2. Of those that a mesh axis runs over, the one named last changes fastest.
Arguments:
- measured_correlations: float32 [16, 2, 8, 2, 128], P(('group', 'tile', 'tm'), 'pol'), parts along dimension 0, may hold values from -6 to 6
- subpixel_coordinates: float32 [16, 8, 2, 128], P(('group', 'tile', 'tm')), parts along dimension 0, may hold values from 0 to 1
- kernel_start_pixel: int32 [16, 8, 128], P(('group', 'tile', 'tm')), parts along dimension 0, may hold values from 0 to 250360, as said below
- antenna_pairs_per_group: int32 [16, 8, 2], P(('group', 'tile', 'tm')), parts along dimension 0, may hold values from 0 to 196, as said below
- group_epoch_number_list: int32 [16, 8], P(('group', 'tile', 'tm')), parts along dimension 0, may hold values from 0 to 1
- occupied_group_tallies: int32 [16, 4], P(('group', 'tile', 'tm')), parts along dimension 0, may hold values from 0 to 2, as said below
- predicted_fourier_plane: bfloat16 [2, 8, 2, 496, 512], P('pol', ('group', 'tile')), parts along dimension 1, may hold values from -6 to 6
- pointing_errors: float32 [2, 4, 256], P(None, 'group'), parts along dimension 1, may hold values from -2.5 to 2.5
Outputs:
- residual: float32 [16, 2, 8, 2, 128], P(('group', 'tile', 'tm'), 'pol'), parts along dimension 0
- gradient: float32 [2, 1024], P(None, ('group', 'tile', 'tm', 'pol')), parts along dimension 1
The draws below stay inside these ranges and needn't reach their ends.
There are 2 independent parts, one for each index of `group`. The reference program is written for one: setup_inputs(seed, part) draws one part's arguments, and reference() takes and returns one part's arrays. A program takes and returns all parts, laid end to end along the dimension named above; each array names one. Nothing has to cross between parts.
Inputs may be any that keep to these rules, and one draw needn't show every extreme that they name: `kernel_start_pixel`: iu * 512 + iv with iu <= 488 and iv <= 504, so the patch lies inside its tile. `antenna_pairs_per_group`: two different antennas of the 197 dishes. Holder h lies on tile-axis index t = h * 4 // 8; occupied_group_tallies[h, (t + 1) mod 4] is 2, occupied_group_tallies[h, (t + 2) mod 4] is 1, and every other tile of h has at most 1 filled slots.
All inputs are finite; a program needn't handle non-finite values.
Results may differ from the reference program's by a relative error of at most 0.0003.
Values sent between devices are 32-bit elements; how exact they have to be, the bound alone decides.
A program may use at most 256 MiB of HBM per device.

```python
import math
import jax
import jax.numpy as jnp
from jax import lax

BLOCK_VISIBILITY = 128
CAP = 2
TU = 496
TV = 512
SUPPORT = 8
DISH_COUNT = 197
DISH_COLUMNS = 256
TIME_SLOTS = 2
HOLDER_COUNT = 8
BLOCK_SLOTS = 8
POLS = 2
N_TILE = 4


def draw_kernel_start_pixel(key, part):
    key = jax.random.fold_in(key, 3)
    leading_key, trailing_key = jax.random.split(key)
    row_cells = jax.random.randint(leading_key, (HOLDER_COUNT, BLOCK_SLOTS, BLOCK_VISIBILITY), 0, TU - SUPPORT + 1)
    col_cells = jax.random.randint(trailing_key, (HOLDER_COUNT, BLOCK_SLOTS, BLOCK_VISIBILITY), 0, TV - SUPPORT + 1)
    packed = row_cells * TV + col_cells
    packed = packed.at[0, 0, 0].set((TU - SUPPORT) * TV + TV - SUPPORT)
    packed = packed.at[0, 0, 1].set(0)
    return packed.astype(jnp.int32)


def draw_antenna_pairs_per_group(key, part):
    key = jax.random.fold_in(key, 5)
    leading_key, trailing_key = jax.random.split(key)
    first_dish = jax.random.randint(leading_key, (HOLDER_COUNT, BLOCK_SLOTS), 0, DISH_COUNT)
    separation = jax.random.randint(trailing_key, (HOLDER_COUNT, BLOCK_SLOTS), 1, DISH_COUNT)
    second_dish = (first_dish + separation) % DISH_COUNT
    paired_values = jnp.stack([first_dish, second_dish], axis=-1).astype(jnp.int32)
    paired_values = paired_values.at[0, 0].set(jnp.array([0, DISH_COUNT - 1], dtype=jnp.int32))
    return paired_values


def draw_occupied_group_tallies(key, part):
    key = jax.random.fold_in(key, 7)
    raw_bits = jax.random.randint(key, (HOLDER_COUNT, N_TILE), 0, 1 << 20)
    filled = raw_bits % (CAP // 2 + 1)
    holder_tile = jnp.arange(HOLDER_COUNT, dtype=jnp.int32) * N_TILE // HOLDER_COUNT
    heavy = (holder_tile + 1) % N_TILE
    second = (holder_tile + 2) % N_TILE
    columns = jnp.arange(N_TILE, dtype=jnp.int32)
    filled = jnp.where(columns[None, :] == second[:, None], CAP // 2, filled)
    return jnp.where(columns[None, :] == heavy[:, None], CAP, filled).astype(jnp.int32)


def touch_ends(values, stream_key, low, top_value):
    spot = [jax.random.randint(jax.random.fold_in(stream_key, axis), (), 0, length) for axis, length in enumerate(values.shape)]
    longest = values.shape.index(max(values.shape))
    neighbour = spot[:longest] + [(spot[longest] + 1) % values.shape[longest]] + spot[longest + 1:]
    return values.at[tuple(spot)].set(low).at[tuple(neighbour)].set(top_value)


def block_levels(own_key, dims, cuts, least, high):
    gain = 1.0
    for axis_at, blocks in cuts:
        draws = jax.random.uniform(jax.random.fold_in(jax.random.fold_in(own_key, 6), axis_at), (blocks,), jnp.float32, least / len(cuts), high / len(cuts))
        gain = gain * jnp.repeat(jnp.exp(draws), dims[axis_at] // blocks).reshape((-1,) + (1,) * (len(dims) - 1 - axis_at))
    return gain


def normal_values(key, shape, deviation, most, shards=(), kind=jnp.bfloat16):
    result = jax.random.normal(key, shape, jnp.float32) * deviation
    if len(shards) > 0:
        result = block_levels(key, shape, shards, -0.22, 0.18) * result
    return jnp.clip(result, min=-most, max=most).astype(kind)


def setup_inputs(seed: int = 0, part: int = 0) -> dict:
    streams_of = jax.random.split(jax.random.key(seed), 9)
    own_keys = jax.random.split(jax.random.fold_in(streams_of[8], part), 9)
    return {
        "measured_correlations": normal_values(own_keys[0], (HOLDER_COUNT, POLS, BLOCK_SLOTS, 2, BLOCK_VISIBILITY), 1.0, 6.0, ((0, 8), (1, 2)), jnp.float32),
        "subpixel_coordinates": jnp.clip(1.0 * jax.random.uniform(own_keys[1], (HOLDER_COUNT, BLOCK_SLOTS, 2, BLOCK_VISIBILITY), jnp.float32) ** block_levels(own_keys[1], (HOLDER_COUNT, BLOCK_SLOTS, 2, BLOCK_VISIBILITY), ((0, 8),), -0.2, 0.2), 0.0, 1.0),
        "kernel_start_pixel": draw_kernel_start_pixel(jax.random.fold_in(jax.random.fold_in(streams_of[8], part), 71), part),
        "antenna_pairs_per_group": draw_antenna_pairs_per_group(jax.random.fold_in(jax.random.fold_in(streams_of[8], part), 71), part),
        "group_epoch_number_list": touch_ends(jax.random.randint(own_keys[4], (HOLDER_COUNT, BLOCK_SLOTS), 0, TIME_SLOTS), jax.random.fold_in(own_keys[4], 1), 0, TIME_SLOTS - 1).astype(jnp.int32),
        "occupied_group_tallies": draw_occupied_group_tallies(jax.random.fold_in(jax.random.fold_in(streams_of[8], part), 71), part),
        "predicted_fourier_plane": normal_values(own_keys[6], (POLS, N_TILE, 2, TU, TV), 1.0, 6.0, ((0, 2), (1, 4))),
        "pointing_errors": normal_values(own_keys[7], (2, TIME_SLOTS, DISH_COLUMNS), 0.6, 2.5, (), jnp.float32),
    }


SHIFT_GAIN = 0.5
BELL_WIDTH = 1.5

def kernel_taper(fraction, shift_cells):
    tap_location = jnp.arange(SUPPORT, dtype=jnp.int32).astype(fraction.dtype) - (SUPPORT - 1) / 2.0
    separation = tap_location[None, None, :] - fraction[:, :, None] - shift_cells[:, None, None]
    bell = jnp.exp(-separation * separation / (2.0 * BELL_WIDTH * BELL_WIDTH))
    return (bell, SHIFT_GAIN * separation / (BELL_WIDTH * BELL_WIDTH) * bell)

def reference(measured_correlations, subpixel_coordinates, kernel_start_pixel, antenna_pairs_per_group, group_epoch_number_list, occupied_group_tallies, predicted_fourier_plane, pointing_errors):
    holder_list = measured_correlations.shape[0]
    polarization_count = measured_correlations.shape[1]
    block_list = measured_correlations.shape[2]
    block_order = jnp.arange(block_list, dtype=jnp.int32)
    tile_of = block_order // CAP
    tap_ids = jnp.arange(SUPPORT, dtype=jnp.int32)
    patch_column = (tap_ids[:, None] * TV + tap_ids[None, :]).reshape(-1)
    flattened_grid = predicted_fourier_plane.reshape(polarization_count, N_TILE, 2, TU * TV)
    key_number = TIME_SLOTS * DISH_COLUMNS

    def holder_terms(container_entry):
        filled = block_order % CAP < occupied_group_tallies[container_entry][tile_of]
        antenna_roster = antenna_pairs_per_group[container_entry]
        current_slot = group_epoch_number_list[container_entry]
        shift_cells = SHIFT_GAIN * (pointing_errors[:, current_slot, antenna_roster[:, 0]] + pointing_errors[:, current_slot, antenna_roster[:, 1]])
        along_u, slope_u = kernel_taper(subpixel_coordinates[container_entry][:, 0], shift_cells[0])
        along_v, slope_v = kernel_taper(subpixel_coordinates[container_entry][:, 1], shift_cells[1])
        shape_out = (block_list, BLOCK_VISIBILITY, SUPPORT * SUPPORT)
        weights = (along_u[:, :, :, None] * along_v[:, :, None, :]).reshape(shape_out)
        weights_u = (slope_u[:, :, :, None] * along_v[:, :, None, :]).reshape(shape_out)
        weights_v = (along_u[:, :, :, None] * slope_v[:, :, None, :]).reshape(shape_out)
        patch_index = kernel_start_pixel[container_entry][:, :, None] + patch_column[None, None, :]
        residual_list = []
        block_terms = jnp.zeros((2, block_list), measured_correlations.dtype)
        for polar in range(polarization_count):
            samples = flattened_grid[polar][tile_of[:, None, None], :, patch_index].astype(measured_correlations.dtype)
            model_vis = lax.optimization_barrier(jnp.sum(weights[..., None] * samples, axis=2))
            deriv_u = lax.optimization_barrier(jnp.sum(weights_u[..., None] * samples, axis=2))
            deriv_v = lax.optimization_barrier(jnp.sum(weights_v[..., None] * samples, axis=2))
            residual = measured_correlations[container_entry, polar] - jnp.transpose(model_vis, (0, 2, 1))
            residual = jnp.where(filled[:, None, None], residual, 0.0)
            term_u = -2.0 * lax.optimization_barrier(jnp.sum(residual * jnp.transpose(deriv_u, (0, 2, 1)), axis=(1, 2)))
            term_v = -2.0 * lax.optimization_barrier(jnp.sum(residual * jnp.transpose(deriv_v, (0, 2, 1)), axis=(1, 2)))
            block_terms = block_terms + jnp.stack([term_u, term_v])
            residual_list.append(residual)
        leading_key = current_slot * DISH_COLUMNS + antenna_roster[:, 0]
        trailing_key = current_slot * DISH_COLUMNS + antenna_roster[:, 1]
        gradient = jnp.zeros((2, key_number), measured_correlations.dtype)
        gradient = gradient.at[:, leading_key].add(block_terms).at[:, trailing_key].add(block_terms)
        return (jnp.stack(residual_list), gradient)
    residuals, gradients = lax.map(holder_terms, jnp.arange(holder_list, dtype=jnp.int32))
    scale_factor = 1.0 / math.sqrt(2.0 * polarization_count * holder_list * block_list * BLOCK_VISIBILITY / DISH_COUNT)
    return (residuals, lax.optimization_barrier(jnp.sum(gradients, axis=0)) * scale_factor)
```

```python
import functools
import math

import jax
import jax.numpy as jnp
from jax import lax
from jax.experimental import pallas as pl
from jax.experimental.pallas import tpu as pltpu
from jax.sharding import PartitionSpec as P

SUPPORT = 8
DISH_COUNT = 197
SHIFT_GAIN = 0.5
BELL_WIDTH = 1.5
AXES = ("group", "tile", "tm", "pol")
MESH = pl.DeviceIdType.MESH


def taps(centre, start):
    row = lax.broadcasted_iota(jnp.int32, (8, start.shape[1]), 0)
    tap = (row - start) & 7
    separation = tap.astype(jnp.float32) - (SUPPORT - 1) / 2.0 - centre
    bell = jnp.exp(-separation * separation / (2.0 * BELL_WIDTH * BELL_WIDTH))
    slope = SHIFT_GAIN * separation / (BELL_WIDTH * BELL_WIDTH) * bell
    return bell, slope, (start + tap) >> 3


def spread(values, hit):
    high = values.astype(jnp.bfloat16).astype(jnp.float32)
    parts = []
    for part in (high, values - high):
        laid = jnp.where(hit, part[None], 0.0)
        parts.append(laid.reshape(-1, laid.shape[2]).astype(jnp.bfloat16))
    return jnp.concatenate(parts, axis=0)


def kernel(
    sizes,
    scale,
    meas_ref,
    sub_ref,
    cell_ref,
    pair_ref,
    epoch_ref,
    tally_ref,
    grid_ref,
    point_ref,
    res_ref,
    grad_ref,
    stage,
    recv,
    out_blocks,
    back,
    part,
    gathered,
    tile_grid,
    grid_sem,
    fwd_send,
    fwd_recv,
    back_send,
    back_recv,
    grad_send,
    grad_recv,
):
    n_tile, n_tm, n_pol = sizes
    count = n_tile * n_tm * n_pol
    group = lax.axis_index("group")
    tile = lax.axis_index("tile")
    tm = lax.axis_index("tm")
    pol = lax.axis_index("pol")
    rows_u, rows_v = grid_ref.shape[3], grid_ref.shape[4]
    width = meas_ref.shape[4]
    columns = point_ref.shape[2]
    own_columns = grad_ref.shape[1]
    slots = n_tile + 1

    load = pltpu.make_async_copy(grid_ref.at[0, 0], tile_grid, grid_sem)
    load.start()

    def peer(k):
        return (
            group,
            lax.rem(tile + k // (n_tm * n_pol), n_tile),
            lax.rem(tm + (k // n_pol) % n_tm, n_tm),
            lax.rem(pol + k % n_pol, n_pol),
        )

    barrier = pltpu.get_barrier_semaphore()

    def greet(k, carry):
        pl.semaphore_signal(barrier, inc=1, device_id=peer(k), device_id_type=MESH)
        return carry

    lax.fori_loop(1, count, greet, 0)

    def block_of(slot):
        if isinstance(slot, int):
            step, half = (slot if slot < 2 else slot - 1), int(slot == 2)
        else:
            step, half = slot - 1, 0
        target = lax.rem(tile + step, n_tile)
        return target, half, 2 * target + half

    def pack(slot):
        target, half, q = block_of(slot)
        time = epoch_ref[0, q]
        first, second = pair_ref[0, q, 0], pair_ref[0, q, 1]
        filled = half < tally_ref[0, target]
        stage[slot, 0:2, :] = meas_ref[0, 0, q]
        sub = sub_ref[0, q]
        for c in range(2):
            shift = SHIFT_GAIN * (point_ref[c, time, first] + point_ref[c, time, second])
            stage[slot, 2 + c : 3 + c, :] = sub[c : c + 1] + shift
        stage[slot, 4:5, :] = cell_ref[0, pl.ds(q, 1), :].astype(jnp.float32)
        for j, antenna in enumerate((first, second)):
            key = jnp.where(filled, time * columns + antenna, -1)
            stage[slot, 5 + j : 6 + j, :] = jnp.full((1, width), key, jnp.int32).astype(jnp.float32)

    def over_slots(body, first):
        for slot in range(first, min(slots, 5)):
            body(slot)
        if slots > 5:
            lax.fori_loop(5, slots, lambda s, c: (body(s), c)[1], 0)

    over_slots(pack, 0)
    part[...] = jnp.zeros_like(part)
    pl.semaphore_wait(barrier, count - 1)

    def first_slot(step):
        return 1 if isinstance(step, int) and step == 1 else step + 1

    def size_of(step):
        return 2 if isinstance(step, int) and step == 1 else 1

    def forward(step):
        span = pl.ds(first_slot(step), size_of(step))
        return pltpu.make_async_remote_copy(
            src_ref=stage.at[span],
            dst_ref=recv.at[span],
            send_sem=fwd_send.at[step],
            recv_sem=fwd_recv.at[step],
            device_id=(group, lax.rem(tile + step, n_tile), tm, pol),
            device_id_type=MESH,
        )

    def backward(step):
        span = pl.ds(first_slot(step), size_of(step))
        return pltpu.make_async_remote_copy(
            src_ref=out_blocks.at[span],
            dst_ref=back.at[span],
            send_sem=back_send.at[step],
            recv_sem=back_recv.at[step],
            device_id=(group, lax.rem(tile - step + n_tile, n_tile), tm, pol),
            device_id_type=MESH,
        )

    def over_steps(body, order=(1, 3, 2)):
        for step in order:
            body(step)
        if n_tile > 4:
            lax.fori_loop(4, n_tile, lambda s, c: (body(s), c)[1], 0)

    over_steps(lambda step: forward(step).start())
    load.wait()

    lane = lax.broadcasted_iota(jnp.int32, part.shape, 2)
    key_here = lax.broadcasted_iota(jnp.int32, part.shape, 0) * own_columns + lane % own_columns
    first_half = lane < own_columns
    inside = lane < 2 * own_columns
    key_here = jnp.where(inside, key_here, -2).astype(jnp.float32)

    def process(source, target_ref, slot):
        block = source[slot]
        cell = block[4:5].astype(jnp.int32)
        start_u, start_v = cell // rows_v, cell % rows_v
        bell_u, slope_u, at_u = taps(block[2:3], start_u)
        bell_v, slope_v, at_v = taps(block[3:4], start_v)
        shape_v = (rows_v // 8, 8, width)
        hit_v = lax.broadcasted_iota(jnp.int32, shape_v, 0) == at_v[None]
        weights = jnp.concatenate([spread(bell_v, hit_v), spread(slope_v, hit_v)], axis=1)
        shape_u = (rows_u // 8, 8, width)
        hit_u = lax.broadcasted_iota(jnp.int32, shape_u, 0) == at_u[None]
        grid = tile_grid[...].reshape(2 * rows_u, rows_v)
        along = jnp.dot(
            jnp.concatenate([grid, grid], axis=1), weights, preferred_element_type=jnp.float32
        )
        residuals = []
        term_u = jnp.zeros((1, width), jnp.float32)
        term_v = jnp.zeros((1, width), jnp.float32)
        for c in range(2):
            rows = along[c * rows_u : (c + 1) * rows_u]
            with_bell = jnp.sum(jnp.where(hit_u, rows[:, :width].reshape(shape_u), 0.0), axis=0)
            with_slope = jnp.sum(jnp.where(hit_u, rows[:, width:].reshape(shape_u), 0.0), axis=0)
            model = jnp.sum(bell_u * with_bell, axis=0, keepdims=True)
            deriv_u = jnp.sum(slope_u * with_bell, axis=0, keepdims=True)
            deriv_v = jnp.sum(bell_u * with_slope, axis=0, keepdims=True)
            residual = block[c : c + 1] - model
            residuals.append(residual)
            term_u = term_u + residual * deriv_u
            term_v = term_v + residual * deriv_v
        target_ref[slot] = jnp.concatenate(residuals, axis=0)
        total_u = -2.0 * jnp.sum(term_u, axis=1, keepdims=True)
        total_v = -2.0 * jnp.sum(term_v, axis=1, keepdims=True)
        hits = (key_here == block[5:6][None]).astype(jnp.float32)
        hits = hits + (key_here == block[6:7][None]).astype(jnp.float32)
        part[...] += hits * jnp.where(first_half, total_u[None], total_v[None])

    process(stage, back, 0)

    def serve(step):
        forward(step).wait_recv()
        for j in range(size_of(step)):
            process(recv, out_blocks, first_slot(step) + j)
        backward(step).start()

    over_steps(serve)

    me = (tile * n_tm + tm) * n_pol + pol

    def hand_out(k, carry):
        where = peer(k)
        row = (where[1] * n_tm + where[2]) * n_pol + where[3]
        pltpu.make_async_remote_copy(
            src_ref=part.at[pl.ds(row, 1)],
            dst_ref=gathered.at[pl.ds(k - 1, 1)],
            send_sem=grad_send,
            recv_sem=grad_recv,
            device_id=where,
            device_id_type=MESH,
        ).start()
        return carry

    lax.fori_loop(1, count, hand_out, 0)

    res_ref[...] = jnp.zeros_like(res_ref)

    def put(slot):
        target, half, q = block_of(slot)
        filled = half < tally_ref[0, target]
        res_ref[0, 0, q] = jnp.where(filled, back[slot], 0.0)

    put(0)

    def collect(step):
        backward(step).wait_recv()
        for j in range(size_of(step)):
            put(first_slot(step) + j)

    over_steps(collect)

    everyone = pltpu.make_async_remote_copy(
        src_ref=gathered,
        dst_ref=gathered,
        send_sem=grad_send,
        recv_sem=grad_recv,
        device_id=peer(1),
        device_id_type=MESH,
    )
    everyone.wait_recv()
    total = (part[pl.ds(me, 1)][0] + jnp.sum(gathered[...], axis=0)) * scale
    grad_ref[0:1, :] = total[:, :own_columns]
    grad_ref[1:2, :] = total[:, own_columns : 2 * own_columns]
    everyone.wait_send()

    def settle(step):
        forward(step).wait_send()
        backward(step).wait_send()

    over_steps(settle)


def solution(mesh):
    sizes = tuple(mesh.shape[name] for name in AXES[1:])
    n_tile, n_tm, n_pol = sizes
    count = n_tile * n_tm * n_pol

    def local(meas, sub, cells, pairs, epochs, tallies, grid, pointing):
        blocks, width = meas.shape[2], meas.shape[4]
        holders = n_tile * n_tm
        scale = 1.0 / math.sqrt(2.0 * n_pol * holders * blocks * width / DISH_COUNT)
        own_columns = pointing.shape[1] * pointing.shape[2] // count
        slots = n_tile + 1
        vmem = pl.BlockSpec(memory_space=pltpu.VMEM)
        smem = pl.BlockSpec(memory_space=pltpu.SMEM)
        dma = pltpu.SemaphoreType.DMA
        return pl.pallas_call(
            functools.partial(kernel, sizes, scale),
            out_shape=(
                jax.ShapeDtypeStruct(meas.shape, jnp.float32),
                jax.ShapeDtypeStruct((2, own_columns), jnp.float32),
            ),
            in_specs=[vmem, vmem, vmem, smem, smem, smem, pl.BlockSpec(memory_space=pl.ANY), smem],
            out_specs=(vmem, vmem),
            scratch_shapes=[
                pltpu.VMEM((slots, 8, width), jnp.float32),
                pltpu.VMEM((slots, 8, width), jnp.float32),
                pltpu.VMEM((slots, 2, width), jnp.float32),
                pltpu.VMEM((slots, 2, width), jnp.float32),
                pltpu.VMEM((count, 1, 128), jnp.float32),
                pltpu.VMEM((count - 1, 1, 128), jnp.float32),
                pltpu.VMEM(grid.shape[2:], jnp.bfloat16),
                dma,
                dma((n_tile,)),
                dma((n_tile,)),
                dma((n_tile,)),
                dma((n_tile,)),
                dma,
                dma,
            ],
            compiler_params=pltpu.CompilerParams(
                collective_id=0, has_side_effects=True, vmem_limit_bytes=48 << 20
            ),
        )(meas, sub, cells, pairs, epochs, tallies, grid, pointing)

    return jax.shard_map(
        local,
        mesh=mesh,
        in_specs=(
            P(("group", "tile", "tm"), "pol", None, None, None),
            P(("group", "tile", "tm"), None, None, None),
            P(("group", "tile", "tm"), None, None),
            P(("group", "tile", "tm"), None, None),
            P(("group", "tile", "tm"), None),
            P(("group", "tile", "tm"), None),
            P("pol", ("group", "tile"), None, None, None),
            P(None, "group", None),
        ),
        out_specs=(
            P(("group", "tile", "tm"), "pol", None, None, None),
            P(None, ("group", "tile", "tm", "pol")),
        ),
        check_vma=False,
    )
```

```python
import functools
import math

import jax
import jax.numpy as jnp
from jax import lax
from jax.experimental import pallas as pl
from jax.experimental.pallas import tpu as pltpu
from jax.sharding import PartitionSpec as P

SUPPORT = 8
DISH_COUNT = 197
SHIFT_GAIN = 0.5
BELL_WIDTH = 1.5
AXES = ("group", "tile", "tm", "pol")
MESH = pl.DeviceIdType.MESH


def taps(centre, start):
    row = lax.broadcasted_iota(jnp.int32, (8, start.shape[1]), 0)
    tap = (row - start) & 7
    separation = tap.astype(jnp.float32) - (SUPPORT - 1) / 2.0 - centre
    bell = jnp.exp(-separation * separation / (2.0 * BELL_WIDTH * BELL_WIDTH))
    slope = SHIFT_GAIN * separation / (BELL_WIDTH * BELL_WIDTH) * bell
    return bell, slope, (start + tap) >> 3


def spread(values, hit):
    high = values.astype(jnp.bfloat16).astype(jnp.float32)
    parts = []
    for part in (high, values - high):
        laid = jnp.where(hit, part[None], 0.0)
        parts.append(laid.reshape(-1, laid.shape[2]).astype(jnp.bfloat16))
    return jnp.concatenate(parts, axis=0)


def kernel(
    sizes,
    scale,
    meas_hbm,
    sub_hbm,
    cell_hbm,
    pair_hbm,
    epoch_hbm,
    tally_hbm,
    grid_ref,
    point_hbm,
    res_ref,
    grad_ref,
    meas_ref,
    sub_ref,
    cell_ref,
    pair_ref,
    epoch_ref,
    tally_ref,
    point_ref,
    stage,
    recv,
    out_blocks,
    back,
    part,
    gathered,
    tile_grid,
    grid_sem,
    load_sem,
    fwd_send,
    fwd_recv,
    back_send,
    back_recv,
    grad_send,
    grad_recv,
):
    n_tile, n_tm, n_pol = sizes
    count = n_tile * n_tm * n_pol
    group = lax.axis_index("group")
    tile = lax.axis_index("tile")
    tm = lax.axis_index("tm")
    pol = lax.axis_index("pol")
    rows_u, rows_v = grid_ref.shape[3], grid_ref.shape[4]
    width = meas_ref.shape[4]
    columns = point_ref.shape[2]
    own_columns = grad_ref.shape[1]
    slots = n_tile + 1

    loads = [
        pltpu.make_async_copy(source, target, load_sem.at[i])
        for i, (source, target) in enumerate(
            (
                (epoch_hbm, epoch_ref),
                (pair_hbm, pair_ref),
                (tally_hbm, tally_ref),
                (point_hbm, point_ref),
                (cell_hbm, cell_ref),
                (sub_hbm, sub_ref),
                (meas_hbm, meas_ref),
            )
        )
    ]
    for copy in loads:
        copy.start()
    load = pltpu.make_async_copy(grid_ref.at[0, 0], tile_grid, grid_sem)
    load.start()

    def ahead(at, step, size):
        after = at + step
        return jnp.where(after >= size, after - size, after)

    def peer(k):
        return (
            group,
            ahead(tile, k // (n_tm * n_pol), n_tile),
            ahead(tm, (k // n_pol) % n_tm, n_tm),
            ahead(pol, k % n_pol, n_pol),
        )

    def over_peers(body):
        if count <= 32:
            for k in range(1, count):
                body(k)
        else:
            lax.fori_loop(1, count, lambda k, c: (body(k), c)[1], 0)

    barrier = pltpu.get_barrier_semaphore()

    def greet(k):
        pl.semaphore_signal(barrier, inc=1, device_id=peer(k), device_id_type=MESH)

    over_peers(greet)

    def block_of(slot):
        if isinstance(slot, int):
            step, half = (slot if slot < 2 else slot - 1), int(slot == 2)
        else:
            step, half = slot - 1, 0
        target = ahead(tile, step, n_tile)
        return target, half, 2 * target + half

    def pack(slot):
        target, half, q = block_of(slot)
        time = epoch_ref[0, q]
        first, second = pair_ref[0, 0, q], pair_ref[0, 1, q]
        filled = half < tally_ref[0, target]
        stage[slot, 0:2, :] = meas_ref[0, 0, q]
        sub = sub_ref[0, q]
        for c in range(2):
            shift = SHIFT_GAIN * (point_ref[c, time, first] + point_ref[c, time, second])
            stage[slot, 2 + c : 3 + c, :] = sub[c : c + 1] + shift
        stage[slot, 4:5, :] = cell_ref[0, pl.ds(q, 1), :].astype(jnp.float32)
        for j, antenna in enumerate((first, second)):
            key = jnp.where(filled, time * columns + antenna, -1)
            stage[slot, 5 + j : 6 + j, :] = jnp.full((1, width), key, jnp.int32).astype(jnp.float32)

    def over_slots(body, first):
        for slot in range(first, min(slots, 5)):
            body(slot)
        if slots > 5:
            lax.fori_loop(5, slots, lambda s, c: (body(s), c)[1], 0)

    for copy in loads:
        copy.wait()
    over_slots(pack, 0)
    part[...] = jnp.zeros_like(part)
    pl.semaphore_wait(barrier, count - 1)

    def first_slot(step):
        return 1 if isinstance(step, int) and step == 1 else step + 1

    def size_of(step):
        return 2 if isinstance(step, int) and step == 1 else 1

    def forward(step):
        span = pl.ds(first_slot(step), size_of(step))
        return pltpu.make_async_remote_copy(
            src_ref=stage.at[span],
            dst_ref=recv.at[span],
            send_sem=fwd_send.at[step],
            recv_sem=fwd_recv.at[step],
            device_id=(group, ahead(tile, step, n_tile), tm, pol),
            device_id_type=MESH,
        )

    def backward(step):
        span = pl.ds(first_slot(step), size_of(step))
        return pltpu.make_async_remote_copy(
            src_ref=out_blocks.at[span],
            dst_ref=back.at[span],
            send_sem=back_send.at[step],
            recv_sem=back_recv.at[step],
            device_id=(group, ahead(tile, n_tile - step, n_tile), tm, pol),
            device_id_type=MESH,
        )

    def over_steps(body, order=(1, 3, 2)):
        for step in order:
            body(step)
        if n_tile > 4:
            lax.fori_loop(4, n_tile, lambda s, c: (body(s), c)[1], 0)

    over_steps(lambda step: forward(step).start())
    load.wait()

    lane = lax.broadcasted_iota(jnp.int32, part.shape, 2)
    key_here = lax.broadcasted_iota(jnp.int32, part.shape, 0) * own_columns + lane % own_columns
    first_half = lane < own_columns
    inside = lane < 2 * own_columns
    key_here = jnp.where(inside, key_here, -2).astype(jnp.float32)

    def process(source, target_ref, slot):
        block = source[slot]
        cell = block[4:5].astype(jnp.int32)
        start_u, start_v = cell // rows_v, cell % rows_v
        bell_u, slope_u, at_u = taps(block[2:3], start_u)
        bell_v, slope_v, at_v = taps(block[3:4], start_v)
        shape_v = (rows_v // 8, 8, width)
        hit_v = lax.broadcasted_iota(jnp.int32, shape_v, 0) == at_v[None]
        weights = jnp.concatenate([spread(bell_v, hit_v), spread(slope_v, hit_v)], axis=1)
        shape_u = (rows_u // 8, 8, width)
        hit_u = lax.broadcasted_iota(jnp.int32, shape_u, 0) == at_u[None]
        grid = tile_grid[...].reshape(2 * rows_u, rows_v)
        along = jnp.dot(
            jnp.concatenate([grid, grid], axis=1), weights, preferred_element_type=jnp.float32
        )
        residuals = []
        term_u = jnp.zeros((1, width), jnp.float32)
        term_v = jnp.zeros((1, width), jnp.float32)
        for c in range(2):
            rows = along[c * rows_u : (c + 1) * rows_u]
            with_bell = jnp.sum(jnp.where(hit_u, rows[:, :width].reshape(shape_u), 0.0), axis=0)
            with_slope = jnp.sum(jnp.where(hit_u, rows[:, width:].reshape(shape_u), 0.0), axis=0)
            model = jnp.sum(bell_u * with_bell, axis=0, keepdims=True)
            deriv_u = jnp.sum(slope_u * with_bell, axis=0, keepdims=True)
            deriv_v = jnp.sum(bell_u * with_slope, axis=0, keepdims=True)
            residual = block[c : c + 1] - model
            residuals.append(residual)
            term_u = term_u + residual * deriv_u
            term_v = term_v + residual * deriv_v
        target_ref[slot] = jnp.concatenate(residuals, axis=0)
        total_u = -2.0 * jnp.sum(term_u, axis=1, keepdims=True)
        total_v = -2.0 * jnp.sum(term_v, axis=1, keepdims=True)
        hits = (key_here == block[5:6][None]).astype(jnp.float32)
        hits = hits + (key_here == block[6:7][None]).astype(jnp.float32)
        part[...] += hits * jnp.where(first_half, total_u[None], total_v[None])

    process(stage, back, 0)

    def serve(step):
        forward(step).wait_recv()
        for j in range(size_of(step)):
            process(recv, out_blocks, first_slot(step) + j)
        backward(step).start()

    over_steps(serve)

    me = (tile * n_tm + tm) * n_pol + pol

    def hand_out(k):
        where = peer(k)
        row = (where[1] * n_tm + where[2]) * n_pol + where[3]
        pltpu.make_async_remote_copy(
            src_ref=part.at[pl.ds(row, 1)],
            dst_ref=gathered.at[pl.ds(k - 1, 1)],
            send_sem=grad_send,
            recv_sem=grad_recv,
            device_id=where,
            device_id_type=MESH,
        ).start()

    over_peers(hand_out)

    res_ref[...] = jnp.zeros_like(res_ref)

    def put(slot):
        target, half, q = block_of(slot)
        filled = half < tally_ref[0, target]
        res_ref[0, 0, q] = jnp.where(filled, back[slot], 0.0)

    put(0)

    def collect(step):
        backward(step).wait_recv()
        for j in range(size_of(step)):
            put(first_slot(step) + j)

    over_steps(collect)

    everyone = pltpu.make_async_remote_copy(
        src_ref=gathered,
        dst_ref=gathered,
        send_sem=grad_send,
        recv_sem=grad_recv,
        device_id=peer(1),
        device_id_type=MESH,
    )
    everyone.wait_recv()
    total = (part[pl.ds(me, 1)][0] + jnp.sum(gathered[...], axis=0)) * scale
    grad_ref[0:1, :] = total[:, :own_columns]
    grad_ref[1:2, :] = total[:, own_columns : 2 * own_columns]
    everyone.wait_send()

    def settle(step):
        forward(step).wait_send()
        backward(step).wait_send()

    over_steps(settle)


def solution(mesh):
    sizes = tuple(mesh.shape[name] for name in AXES[1:])
    n_tile, n_tm, n_pol = sizes
    count = n_tile * n_tm * n_pol

    def local(meas, sub, cells, pairs, epochs, tallies, grid, pointing):
        blocks, width = meas.shape[2], meas.shape[4]
        holders = n_tile * n_tm
        scale = 1.0 / math.sqrt(2.0 * n_pol * holders * blocks * width / DISH_COUNT)
        own_columns = pointing.shape[1] * pointing.shape[2] // count
        slots = n_tile + 1
        vmem = pl.BlockSpec(memory_space=pltpu.VMEM)
        hbm = pl.BlockSpec(memory_space=pltpu.HBM)
        pairs = jnp.swapaxes(pairs, 1, 2)
        dma = pltpu.SemaphoreType.DMA
        return pl.pallas_call(
            functools.partial(kernel, sizes, scale),
            out_shape=(
                jax.ShapeDtypeStruct(meas.shape, jnp.float32),
                jax.ShapeDtypeStruct((2, own_columns), jnp.float32),
            ),
            in_specs=[hbm] * 8,
            out_specs=(vmem, vmem),
            scratch_shapes=[
                pltpu.VMEM(meas.shape, jnp.float32),
                pltpu.VMEM(sub.shape, jnp.float32),
                pltpu.VMEM(cells.shape, jnp.int32),
                pltpu.SMEM(pairs.shape, jnp.int32),
                pltpu.SMEM(epochs.shape, jnp.int32),
                pltpu.SMEM(tallies.shape, jnp.int32),
                pltpu.SMEM(pointing.shape, jnp.float32),
                pltpu.VMEM((slots, 8, width), jnp.float32),
                pltpu.VMEM((slots, 8, width), jnp.float32),
                pltpu.VMEM((slots, 2, width), jnp.float32),
                pltpu.VMEM((slots, 2, width), jnp.float32),
                pltpu.VMEM((count, 1, 128), jnp.float32),
                pltpu.VMEM((count - 1, 1, 128), jnp.float32),
                pltpu.VMEM(grid.shape[2:], jnp.bfloat16),
                dma,
                dma((7,)),
                dma((n_tile,)),
                dma((n_tile,)),
                dma((n_tile,)),
                dma((n_tile,)),
                dma,
                dma,
            ],
            compiler_params=pltpu.CompilerParams(
                collective_id=0, has_side_effects=True, vmem_limit_bytes=60 << 20
            ),
        )(meas, sub, cells, pairs, epochs, tallies, grid, pointing)

    return jax.shard_map(
        local,
        mesh=mesh,
        in_specs=(
            P(("group", "tile", "tm"), "pol", None, None, None),
            P(("group", "tile", "tm"), None, None, None),
            P(("group", "tile", "tm"), None, None),
            P(("group", "tile", "tm"), None, None),
            P(("group", "tile", "tm"), None),
            P(("group", "tile", "tm"), None),
            P("pol", ("group", "tile"), None, None, None),
            P(None, "group", None),
        ),
        out_specs=(
            P(("group", "tile", "tm"), "pol", None, None, None),
            P(None, ("group", "tile", "tm", "pol")),
        ),
        check_vma=False,
    )
```
